32 devices in a mesh: member: 4 (over y, x), space: 8 (over z, core).
Axes of the slice: x: 2, y: 2, z: 4, core: 2. Of those that a mesh axis runs over, the one named last changes fastest.
Arguments:
- state: bfloat16 [8, 4, 16, 256, 1024], P('member', None, None, 'space'), may hold values from -4 to 4
Outputs:
- stepped: bfloat16 [8, 4, 16, 256, 1024], P('member', None, None, 'space')
- correlation: float32 [16, 256, 1024], P(None, 'space', 'member')
The draws below stay inside these ranges and needn't reach their ends.
All inputs are finite; a program needn't handle non-finite values.
Results may differ from the reference program's by a relative error of at most 0.0041.
Values may be sent and summed in bfloat16 or wider, within the bound.
A program may use at most 320 MiB of HBM per device.

```python
import jax
import jax.numpy as jnp
from jax import lax

NY = 1024
LEV = 16
STEPS = 1
MEMBERS = 8
NX = 256


def steps_of(rng, shape, shards, least, top_value):
    def one(axis_at, parts):
        heights = jax.random.uniform(jax.random.fold_in(jax.random.fold_in(rng, 6), axis_at), (parts,), jnp.float32, least / len(shards), top_value / len(shards))
        return jnp.repeat(jnp.exp(heights), shape[axis_at] // parts).reshape((-1,) + (1,) * (len(shape) - axis_at - 1))

    level = one(*shards[0])
    for cut in shards[1:]:
        level = level * one(*cut)
    return level


def noise(rng, dims, width, most, pieces=(), held_as=jnp.bfloat16):
    entries = jax.random.normal(rng, dims, jnp.float32) * width
    if len(pieces) > 0:
        entries = steps_of(rng, dims, pieces, -0.22, 0.18) * entries
    return jnp.clip(entries, min=-most, max=most).astype(held_as)


def setup_inputs(seed: int = 0) -> dict:
    streams_of = jax.random.split(jax.random.key(seed), 2)
    return {
        "state": noise(streams_of[0], (MEMBERS, 4, LEV, NX, NY), 1.0, 4.0, ((0, 4), (3, 8))),
    }


time_step = 0.2
viscosity = 0.1
var_floor = 0.25

def advance(padded):
    whole = padded.astype(jnp.float32)
    center = whole[..., 2:-2, :]
    dxf = (8.0 * (whole[..., 3:-1, :] - whole[..., 1:-3, :]) - (whole[..., 4:, :] - whole[..., :-4, :])) / 12.0
    yplus = jnp.roll(center, -1, -1)
    yminus = jnp.roll(center, 1, -1)
    dyf = (8.0 * (yplus - yminus) - (jnp.roll(center, -2, -1) - jnp.roll(center, 2, -1))) / 12.0
    zpad = jnp.pad(center, [(0, 0)] * (center.ndim - 3) + [(1, 1), (0, 0), (0, 0)])
    zup = zpad[..., 2:, :, :]
    zdown = zpad[..., :-2, :, :]
    dzf = (zup - zdown) * 0.5
    lap = whole[..., 3:-1, :] + whole[..., 1:-3, :] + yplus + yminus + zup + zdown - 6.0 * center
    uvel = center[..., 0:1, :, :, :]
    vvel = center[..., 1:2, :, :, :]
    wvel = center[..., 2:3, :, :, :]
    buoy = center[..., 3:4, :, :, :]
    tend = viscosity * lap - (uvel * dxf + vvel * dyf + wvel * dzf)
    force = jnp.concatenate([jnp.zeros_like(buoy), jnp.zeros_like(buoy), buoy, -wvel], axis=-4)
    return (center + time_step * (tend + force)).astype(jnp.bfloat16)

def correlate(sums, count):
    mean_b = sums[0] / count
    mean_w = sums[1] / count
    var_b = sums[2] / count - mean_b * mean_b
    var_w = sums[3] / count - mean_w * mean_w
    cov = sums[4] / count - mean_b * mean_w
    return cov / jnp.sqrt(jnp.maximum(var_b, var_floor) * jnp.maximum(var_w, var_floor))

def reference(state):

    def one_member(fields):
        current = fields
        for step in range(STEPS):
            padded = jnp.concatenate([current[..., -2:, :], current, current[..., :2, :]], axis=-2)
            current = advance(padded)
        return current
    stepped = lax.map(one_member, state)
    wvel = stepped[:, 2].astype(jnp.float32)
    buoy = stepped[:, 3].astype(jnp.float32)
    sums = jnp.stack([lax.optimization_barrier(jnp.sum(buoy, 0)), lax.optimization_barrier(jnp.sum(wvel, 0)), lax.optimization_barrier(jnp.sum(buoy * buoy, 0)), lax.optimization_barrier(jnp.sum(wvel * wvel, 0)), lax.optimization_barrier(jnp.sum(buoy * wvel, 0))])
    return (stepped, correlate(sums, jnp.float32(MEMBERS)))
```

```python
import functools

import jax
import jax.numpy as jnp
import numpy as np
from jax import lax
from jax.experimental import pallas as pl
from jax.experimental.pallas import tpu as pltpu
from jax.sharding import PartitionSpec as P

time_step = 0.2
viscosity = 0.1
var_floor = 0.25
depth = 4


def stencil_matrix(levels, rows):
    chunks = levels // depth
    inner = (depth + 2) * rows
    a = np.zeros((chunks, 3, depth, rows, inner + 4 * levels), np.float32)

    def column(c, z, x):
        if x < 0:
            return inner + (c * depth + z) * 2 + x + 2
        if x >= rows:
            return inner + 2 * levels + (c * depth + z) * 2 + x - rows
        return (z + 1) * rows + x

    for c in range(chunks):
        for z in range(depth):
            for x in range(rows):
                for d, coef in ((1, 8), (-1, -8), (2, -1), (-2, 1)):
                    a[c, 0, z, x, column(c, z, x + d)] += coef
                a[c, 2, z, x, column(c, z, x + 1)] += 1
                a[c, 2, z, x, column(c, z, x - 1)] += 1
                a[c, 2, z, x, column(c, z, x)] -= 6
                for d in (1, -1):
                    if 0 <= c * depth + z + d < levels:
                        a[c, 1, z, x, (z + 1 + d) * rows + x] += d
                        a[c, 2, z, x, (z + 1 + d) * rows + x] += 1
    return a.reshape(chunks, 3 * depth * rows, -1).astype(jnp.bfloat16)


def step_kernel(first, parts, me_ref, a_ref, main, below, above, halo_lo, halo_hi, *rest):
    if first == 0:
        rest = rest[1:]
    out = rest[0]
    sends = rest[1:-1]
    res = rest[-1]
    rows, cols = main.shape[3], main.shape[4]
    half = 16
    per = rows // half
    for k in range(2):
        f = first + k
        w = jnp.concatenate(
            [below[0, k, 0]]
            + [main[0, f, z] for z in range(depth)]
            + [above[0, k, 0], halo_lo[0, k], halo_hi[0, k]],
            axis=0,
        )
        res[...] = jnp.dot(a_ref[0], w, preferred_element_type=jnp.float32)

        def tile(i, carry):
            z = i // per
            x = pl.multiple_of((i % per) * half, half)
            at = pl.multiple_of(i * half, half)
            span = depth * rows
            get = lambda g: main[0, g, z, pl.ds(x, half), :].astype(jnp.float32)
            u, v, wv = get(0), get(1), get(2)
            cen = get(f)
            dx = res[pl.ds(at, half), :]
            dz = res[pl.ds(span + at, half), :]
            lap = res[pl.ds(2 * span + at, half), :]
            yp = pltpu.roll(cen, cols - 1, 1)
            ym = pltpu.roll(cen, 1, 1)
            yp2 = pltpu.roll(cen, cols - 2, 1)
            ym2 = pltpu.roll(cen, 2, 1)
            dy = 8.0 * (yp - ym) - (yp2 - ym2)
            lap = lap + (yp + ym)
            s = time_step / 12.0
            new = cen + (time_step * viscosity) * lap - (s * (u * dx + v * dy) + (0.5 * time_step) * (wv * dz))
            if f == 2:
                new = new + time_step * get(3)
            elif f == 3:
                new = new - time_step * wv
            out[0, k, z, pl.ds(x, half), :] = new.astype(jnp.bfloat16)
            return carry

        lax.fori_loop(0, depth * per, tile, 0)
        part = cols // parts
        for j, send in enumerate(sends):
            q = me_ref[j]
            send[0, k] = out[0, k, :, :, pl.ds(pl.multiple_of(q * part, part), part)]


def run_step(first, parts, order, a, state, lo, hi, prior=None):
    m_, _, levels, rows, cols = state.shape
    chunks = levels // depth
    fb = first // 2
    sds = jax.ShapeDtypeStruct
    in_specs = [
        pl.BlockSpec((1,) + a.shape[1:], lambda m, c, me: (c, 0, 0)),
        pl.BlockSpec((1, 4, depth, rows, cols), lambda m, c, me: (m, 0, c, 0, 0)),
        pl.BlockSpec((1, 2, 1, rows, cols), lambda m, c, me: (m, fb, jnp.maximum(c * depth - 1, 0), 0, 0)),
        pl.BlockSpec((1, 2, 1, rows, cols), lambda m, c, me: (m, fb, jnp.minimum(c * depth + depth, levels - 1), 0, 0)),
        pl.BlockSpec((1, 2, 2 * levels, cols), lambda m, c, me: (m, fb, 0, 0)),
        pl.BlockSpec((1, 2, 2 * levels, cols), lambda m, c, me: (m, fb, 0, 0)),
    ]
    args = [order, a, state, state, state, lo, hi]
    out_shape = [sds(state.shape, state.dtype)]
    out_specs = [pl.BlockSpec((1, 2, depth, rows, cols), lambda m, c, me: (m, fb, c, 0, 0))]
    alias = {}
    if prior is not None:
        alias = {len(args): 0}
        args.append(prior)
        in_specs.append(pl.BlockSpec(memory_space=pl.ANY))
    else:
        for _ in range(parts):
            out_shape.append(sds((m_, 2, levels, rows, cols // parts), state.dtype))
            out_specs.append(pl.BlockSpec((1, 2, depth, rows, cols // parts), lambda m, c, me: (m, 0, c, 0, 0)))
    return pl.pallas_call(
        functools.partial(step_kernel, first, parts),
        out_shape=out_shape,
        grid_spec=pltpu.PrefetchScalarGridSpec(
            num_scalar_prefetch=1,
            grid=(m_, chunks),
            in_specs=in_specs,
            out_specs=out_specs,
            scratch_shapes=[pltpu.VMEM((3 * depth * rows, cols), jnp.float32)],
        ),
        input_output_aliases=alias,
        compiler_params=pltpu.CompilerParams(vmem_limit_bytes=40 * 2**20),
        cost_estimate=pl.CostEstimate(flops=20 * 10**9, bytes_accessed=16 * 2**20, transcendentals=0),
    )(*args)


def correlate_kernel(count, *refs):
    out = refs[-1]
    for z in range(out.shape[0]):
        sb = sw = sbb = sww = sbw = None
        for ref in refs[:-1]:
            for m in range(ref.shape[0]):
                w = ref[m, 0, z].astype(jnp.float32)
                b = ref[m, 1, z].astype(jnp.float32)
                if sb is None:
                    sb, sw, sbb, sww, sbw = b, w, b * b, w * w, b * w
                else:
                    sb, sw, sbb, sww, sbw = sb + b, sw + w, sbb + b * b, sww + w * w, sbw + b * w
        inv = 1.0 / count
        mb, mw = sb * inv, sw * inv
        vb = sbb * inv - mb * mb
        vw = sww * inv - mw * mw
        cov = sbw * inv - mb * mw
        out[z] = cov * lax.rsqrt(jnp.maximum(vb, var_floor) * jnp.maximum(vw, var_floor))


def run_correlate(count, blocks):
    m_, _, levels, rows, part = blocks[0].shape
    return pl.pallas_call(
        functools.partial(correlate_kernel, count),
        out_shape=jax.ShapeDtypeStruct((levels, rows, part), jnp.float32),
        grid=(levels // depth,),
        in_specs=[pl.BlockSpec((m_, 2, depth, rows, part), lambda c: (0, 0, c, 0, 0))] * len(blocks),
        out_specs=pl.BlockSpec((depth, rows, part), lambda c: (c, 0, 0)),
        compiler_params=pltpu.CompilerParams(vmem_limit_bytes=40 * 2**20),
        cost_estimate=pl.CostEstimate(flops=10**8, bytes_accessed=5 * 2**20, transcendentals=0),
    )(*blocks)


def partner(i, k, parts):
    if parts & (parts - 1) == 0:
        return i ^ k
    return (i + k) % parts


def on_device(parts, count, state):
    m_, _, levels, rows, cols = state.shape
    a = jnp.asarray(stencil_matrix(levels, rows))
    head = state[:, :, :, :2, :].reshape(m_, 4, 2 * levels, cols)
    tail = state[:, :, :, rows - 2 :, :].reshape(m_, 4, 2 * levels, cols)
    lo = lax.ppermute(tail, "space", [(i, (i + 1) % count) for i in range(count)])
    hi = lax.ppermute(head, "space", [((i + 1) % count, i) for i in range(count)])
    me = lax.axis_index("member")
    order = jnp.stack([jnp.asarray(partner(me, k, parts), jnp.int32) for k in range(parts)])
    stepped, *blocks = run_step(2, parts, order, a, state, lo, hi)
    got = [blocks[0]]
    for k in range(1, parts):
        got.append(lax.ppermute(blocks[k], "member", [(i, partner(i, k, parts)) for i in range(parts)]))
    (stepped,) = run_step(0, parts, order, a, state, lo, hi, stepped)
    return stepped, run_correlate(float(m_ * parts), got)


def solution(mesh):
    in_specs = (P("member", None, None, "space", None),)
    out_specs = (P("member", None, None, "space", None), P(None, "space", "member"))
    return jax.shard_map(
        functools.partial(on_device, mesh.shape["member"], mesh.shape["space"]),
        mesh=mesh, in_specs=in_specs, out_specs=out_specs, check_vma=False,
    )
```

```python
import functools

import jax
import jax.numpy as jnp
import numpy as np
from jax import lax
from jax.experimental import pallas as pl
from jax.experimental.pallas import tpu as pltpu
from jax.sharding import PartitionSpec as P

time_step = 0.2
viscosity = 0.1
var_floor = 0.25
depth = 4
edge = 8
vmem = 56 * 2**20


def stencil_matrix(levels, rows, spans, halos):
    chunks = levels // depth
    inner = (depth + 2) * rows
    xs = [x for start, stop in spans for x in range(start, stop)]
    a = np.zeros((chunks, 3, depth, len(xs), inner + (4 * levels if halos else 0)), np.float32)

    def column(c, z, x):
        if x < 0:
            return inner + (c * depth + z) * 2 + x + 2
        if x >= rows:
            return inner + 2 * levels + (c * depth + z) * 2 + x - rows
        return (z + 1) * rows + x

    for c in range(chunks):
        for z in range(depth):
            for n, x in enumerate(xs):
                for d, coef in ((1, 8), (-1, -8), (2, -1), (-2, 1)):
                    a[c, 0, z, n, column(c, z, x + d)] += coef
                a[c, 2, z, n, column(c, z, x + 1)] += 1
                a[c, 2, z, n, column(c, z, x - 1)] += 1
                a[c, 2, z, n, column(c, z, x)] -= 6
                for d in (1, -1):
                    if 0 <= c * depth + z + d < levels:
                        a[c, 1, z, n, (z + 1 + d) * rows + x] += d
                        a[c, 2, z, n, (z + 1 + d) * rows + x] += 1
    return jnp.asarray(a.reshape(chunks, 3 * depth * len(xs), -1).astype(jnp.bfloat16))


def step_kernel(kind, first, parts, spans, me_ref, a_ref, main, below, above, *rest):
    rest = list(rest)
    halos = [rest.pop(0), rest.pop(0)] if kind != "mid" else []
    mid = rest.pop(0) if kind == "edge" else None
    res = rest.pop()
    held = rest.pop() if kind == "edge" else None
    if kind == "edge":
        out, sends = rest[-1 - parts], rest[-parts:]
    elif kind == "mid":
        out, sends = rest[0], rest[1:]
    else:
        out, sends = rest[-1], []
    rows, cols = main.shape[3], main.shape[4]
    count = sum(stop - start for start, stop in spans)
    total = depth * count
    for k in range(2):
        f = first + k
        w = jnp.concatenate(
            [below[0, k, 0]] + [main[0, f, z] for z in range(depth)] + [above[0, k, 0]] + [h[0, k] for h in halos],
            axis=0,
        )
        res[...] = jnp.dot(a_ref[0], w, preferred_element_type=jnp.float32)

        def level(z, carry):
            def get(g, start, stop):
                if kind == "rest":
                    return main[0, g, z, start:stop, :].astype(jnp.float32)
                return main[0, g, z].astype(jnp.float32)[start:stop]

            news = []
            at = 0
            for start, stop in spans:
                base = pl.multiple_of(z * count, 16) + at
                at += stop - start
                u, v, wv = get(0, start, stop), get(1, start, stop), get(2, start, stop)
                cen = get(f, start, stop)
                size = stop - start
                dx = res[pl.ds(pl.multiple_of(base, 8), size), :]
                dz = res[pl.ds(pl.multiple_of(total + base, 8), size), :]
                lap = res[pl.ds(pl.multiple_of(2 * total + base, 8), size), :]
                yp = pltpu.roll(cen, cols - 1, 1)
                ym = pltpu.roll(cen, 1, 1)
                yp2 = pltpu.roll(cen, cols - 2, 1)
                ym2 = pltpu.roll(cen, 2, 1)
                dy = 8.0 * (yp - ym) - (yp2 - ym2)
                lap = lap + (yp + ym)
                s = time_step / 12.0
                new = cen + (time_step * viscosity) * lap - (s * (u * dx + v * dy) + (0.5 * time_step) * (wv * dz))
                if f == 2:
                    new = new + time_step * get(3, start, stop)
                elif f == 3:
                    new = new - time_step * wv
                if kind == "rest":
                    out[0, k, z, start:stop, :] = new.astype(jnp.bfloat16)
                news.append(new)
            if kind == "mid":
                out[0, k, z] = jnp.concatenate(news, axis=0).astype(jnp.bfloat16)
            elif kind == "edge":
                held[z] = jnp.concatenate(news, axis=0).astype(jnp.bfloat16)
                inner = mid[0, k, z].astype(jnp.float32)
                out[0, k, z] = jnp.concatenate([news[0], inner, news[1]], axis=0).astype(jnp.bfloat16)
            return carry

        lax.fori_loop(0, depth, level, 0)
        part = cols // parts
        for j, send in enumerate(sends):
            at = pl.ds(pl.multiple_of(me_ref[j] * part, part), part)
            send[0, k] = held[:, :, at] if kind == "edge" else out[0, k, :, :, at]


def run_step(kind, first, members, parts, spans, order, state, lo=None, hi=None, mid=None, prior=None):
    _, _, levels, rows, cols = state.shape
    chunks = levels // depth
    fb = first // 2
    m0, m1 = members
    a = stencil_matrix(levels, rows, spans, kind != "mid")
    count = sum(stop - start for start, stop in spans)
    sds = jax.ShapeDtypeStruct
    in_specs = [
        pl.BlockSpec((1,) + a.shape[1:], lambda m, c, me: (c, 0, 0)),
        pl.BlockSpec((1, 4, depth, rows, cols), lambda m, c, me: (m + m0, 0, c, 0, 0)),
        pl.BlockSpec((1, 2, 1, rows, cols), lambda m, c, me: (m + m0, fb, jnp.maximum(c * depth - 1, 0), 0, 0)),
        pl.BlockSpec((1, 2, 1, rows, cols), lambda m, c, me: (m + m0, fb, jnp.minimum(c * depth + depth, levels - 1), 0, 0)),
    ]
    args = [order, a, state, state, state]
    if kind != "mid":
        in_specs += [pl.BlockSpec((1, 2, 2 * levels, cols), lambda m, c, me: (m + m0, fb, 0, 0))] * 2
        args += [lo, hi]
    if kind == "edge":
        in_specs.append(pl.BlockSpec((1, 2, depth, rows - count, cols), lambda m, c, me: (m, 0, c, 0, 0)))
        args.append(mid)
    alias = {}
    if prior is not None:
        alias = {len(args): 0}
        args.append(prior)
        in_specs.append(pl.BlockSpec(memory_space=pl.ANY))
    if kind == "mid":
        out_shape = [sds((m1 - m0, 2, levels, count, cols), state.dtype)]
        out_specs = [pl.BlockSpec((1, 2, depth, count, cols), lambda m, c, me: (m, 0, c, 0, 0))]
    else:
        out_shape = [sds(state.shape, state.dtype)]
        out_specs = [pl.BlockSpec((1, 2, depth, rows, cols), lambda m, c, me: (m + m0, fb, c, 0, 0))]
    if kind != "rest":
        out_shape += [sds((m1 - m0, 2, levels, count, cols // parts), state.dtype)] * parts
        out_specs += [pl.BlockSpec((1, 2, depth, count, cols // parts), lambda m, c, me: (m, 0, c, 0, 0))] * parts
    scratch = [pltpu.VMEM((3 * depth * count, cols), jnp.float32)]
    if kind == "edge":
        scratch.insert(0, pltpu.VMEM((depth, count, cols), jnp.bfloat16))
    share = (m1 - m0) * count
    return pl.pallas_call(
        functools.partial(step_kernel, kind, first, parts, spans),
        out_shape=out_shape,
        grid_spec=pltpu.PrefetchScalarGridSpec(
            num_scalar_prefetch=1, grid=(m1 - m0, chunks), in_specs=in_specs, out_specs=out_specs, scratch_shapes=scratch
        ),
        input_output_aliases=alias,
        compiler_params=pltpu.CompilerParams(vmem_limit_bytes=vmem),
        cost_estimate=pl.CostEstimate(flops=share * 4 * 10**8, bytes_accessed=share * 2**18, transcendentals=0),
    )(*args)


def correlate_kernel(count, *refs):
    out = refs[-1]
    n = (len(refs) - 1) // 2
    inv = 1.0 / count

    def rows_of(blocks, z):
        sums = None
        for ref in blocks:
            for m in range(ref.shape[0]):
                w = ref[m, 0, z].astype(jnp.float32)
                b = ref[m, 1, z].astype(jnp.float32)
                terms = (b, w, b * b, w * w, b * w)
                sums = terms if sums is None else [p + q for p, q in zip(sums, terms)]
        mb, mw = sums[0] * inv, sums[1] * inv
        vb = sums[2] * inv - mb * mb
        vw = sums[3] * inv - mw * mw
        cov = sums[4] * inv - mb * mw
        return cov * lax.rsqrt(jnp.maximum(vb, var_floor) * jnp.maximum(vw, var_floor))

    for z in range(out.shape[0]):
        inner = rows_of(refs[:n], z)
        outer = rows_of(refs[n:-1], z)
        out[z] = jnp.concatenate([outer[:edge], inner, outer[edge:]], axis=0)


def run_correlate(count, mids, edges):
    _, _, levels, middle, part = mids[0].shape
    rows = middle + 2 * edge
    specs = [pl.BlockSpec(b.shape[:2] + (depth,) + b.shape[3:], lambda c: (0, 0, c, 0, 0)) for b in mids + edges]
    return pl.pallas_call(
        functools.partial(correlate_kernel, count),
        out_shape=jax.ShapeDtypeStruct((levels, rows, part), jnp.float32),
        grid=(levels // depth,),
        in_specs=specs,
        out_specs=pl.BlockSpec((depth, rows, part), lambda c: (c, 0, 0)),
        compiler_params=pltpu.CompilerParams(vmem_limit_bytes=vmem),
        cost_estimate=pl.CostEstimate(flops=10**8, bytes_accessed=5 * 2**20, transcendentals=0),
    )(*mids, *edges)


def partner(i, k, parts):
    if parts & (parts - 1) == 0:
        return i ^ k
    return (i + k) % parts


def on_device(parts, count, state):
    m_, _, levels, rows, cols = state.shape
    head = state[:, :, :, :2, :].reshape(m_, 4, 2 * levels, cols)
    tail = state[:, :, :, rows - 2 :, :].reshape(m_, 4, 2 * levels, cols)
    lo = lax.ppermute(tail, "space", [(i, (i + 1) % count) for i in range(count)])
    hi = lax.ppermute(head, "space", [((i + 1) % count, i) for i in range(count)])
    me = lax.axis_index("member")
    order = jnp.stack([jnp.asarray(partner(me, k, parts), jnp.int32) for k in range(parts)])

    def exchange(blocks):
        got = [blocks[0]]
        for k in range(1, parts):
            got.append(lax.ppermute(blocks[k], "member", [(i, partner(i, k, parts)) for i in range(parts)]))
        return got

    inner = ((edge, rows - edge),)
    outer = ((0, edge), (rows - edge, rows))
    halves = tuple((x, x + 16) for x in range(0, rows, 16))
    middles, mids, edges = [], [], []
    for m in range(m_):
        middle, *blocks = run_step("mid", 2, (m, m + 1), parts, inner, order, state)
        middles.append(middle)
        mids += exchange(blocks)
    stepped = None
    for m in range(m_):
        stepped, *blocks = run_step("edge", 2, (m, m + 1), parts, outer, order, state, lo, hi, middles[m], stepped)
        edges += exchange(blocks)
    (stepped,) = run_step("rest", 0, (0, m_), parts, halves, order, state, lo, hi, None, stepped)
    return stepped, run_correlate(float(m_ * parts), mids, edges)


def solution(mesh):
    in_specs = (P("member", None, None, "space", None),)
    out_specs = (P("member", None, None, "space", None), P(None, "space", "member"))
    return jax.shard_map(
        functools.partial(on_device, mesh.shape["member"], mesh.shape["space"]),
        mesh=mesh, in_specs=in_specs, out_specs=out_specs, check_vma=False,
    )
```

```python
import functools

import jax
import jax.numpy as jnp
import numpy as np
from jax import lax
from jax.experimental import pallas as pl
from jax.experimental.pallas import tpu as pltpu
from jax.sharding import PartitionSpec as P

time_step = 0.2
viscosity = 0.1
var_floor = 0.25
depth = 4
edge = 8
wide = 256
vmem = 50 * 2**20


def stencil_matrix(levels, rows, spans, halos):
    chunks = levels // depth
    inner = (depth + 2) * rows
    xs = [x for start, stop in spans for x in range(start, stop)]
    a = np.zeros((chunks, 3, depth, len(xs), inner + (4 * levels if halos else 0)), np.float32)

    def column(c, z, x):
        if x < 0:
            return inner + (c * depth + z) * 2 + x + 2
        if x >= rows:
            return inner + 2 * levels + (c * depth + z) * 2 + x - rows
        return (z + 1) * rows + x

    for c in range(chunks):
        for z in range(depth):
            for n, x in enumerate(xs):
                for d, coef in ((1, 8), (-1, -8), (2, -1), (-2, 1)):
                    a[c, 0, z, n, column(c, z, x + d)] += coef
                a[c, 2, z, n, column(c, z, x + 1)] += 1
                a[c, 2, z, n, column(c, z, x - 1)] += 1
                a[c, 2, z, n, column(c, z, x)] += 44
                for d in (1, -1):
                    if 0 <= c * depth + z + d < levels:
                        a[c, 1, z, n, (z + 1 + d) * rows + x] += 6 * d
                        a[c, 2, z, n, (z + 1 + d) * rows + x] += 1
    return jnp.asarray(a.reshape(chunks, 3 * depth * len(xs), -1).astype(jnp.bfloat16))


def column_matrix():
    b = np.zeros((2 * wide, 2 * wide), np.float32)
    for n in range(wide):
        for d, coef in ((1, 8), (-1, -8), (2, -1), (-2, 1)):
            y = n + d
            row = y + wide + 128 if y < 0 else y if y < wide else y + 128
            b[row, n] += coef
            if d * d == 1:
                b[row, wide + n] += 1
    return jnp.asarray(b.astype(jnp.bfloat16))


def step_kernel(kind, first, parts, spans, me_ref, a_ref, b_ref, main, below, above, *rest):
    rest = list(rest)
    halos = [rest.pop(0), rest.pop(0)] if kind != "mid" else []
    mid = rest.pop(0) if kind == "edge" else None
    resy = rest.pop()
    res = rest.pop()
    held = rest.pop() if kind == "edge" else None
    if kind == "edge":
        out, sends = rest[-1 - parts], rest[-parts:]
    elif kind == "mid":
        out, sends = rest[0], rest[1:]
    else:
        out, sends = rest[-1], []
    rows, cols = main.shape[3], main.shape[4]
    count = sum(stop - start for start, stop in spans)
    total = depth * count
    for k in range(2):
        f = first + k
        m = jnp.concatenate([main[0, f, z] for z in range(depth)], axis=0)
        w = jnp.concatenate([below[0, k, 0], m, above[0, k, 0]] + [h[0, k] for h in halos], axis=0)
        res[...] = jnp.dot(a_ref[0], w, preferred_element_type=jnp.float32)
        for j in range(cols // wide):
            lo = (j * wide - 128) % cols
            hi = (j * wide + wide) % cols
            block = jnp.concatenate([m[:, j * wide : (j + 1) * wide], m[:, lo : lo + 128], m[:, hi : hi + 128]], axis=1)
            resy[:, 2 * j * wide : 2 * (j + 1) * wide] = jnp.dot(block, b_ref[...], preferred_element_type=jnp.float32)

        def level(z, carry):
            for j in range(cols // wide):
                seg = slice(j * wide, (j + 1) * wide)

                def get(g, start, stop):
                    if kind == "rest":
                        return main[0, g, z, start:stop, seg].astype(jnp.float32)
                    return main[0, g, z, :, seg].astype(jnp.float32)[start:stop]

                news = []
                at = 0
                for start, stop in spans:
                    base = pl.multiple_of(z * count + at, 8)
                    row = pl.multiple_of(z * rows + start, 8)
                    size = stop - start
                    at += size
                    u, v, wv = get(0, start, stop), get(1, start, stop), get(2, start, stop)
                    dx = res[pl.ds(base, size), seg]
                    dz = res[pl.ds(pl.multiple_of(total + base, 8), size), seg]
                    lap = res[pl.ds(pl.multiple_of(2 * total + base, 8), size), seg]
                    dy = resy[pl.ds(row, size), 2 * j * wide : (2 * j + 1) * wide]
                    lap = lap + resy[pl.ds(row, size), (2 * j + 1) * wide : (2 * j + 2) * wide]
                    new = (time_step * viscosity) * lap - (time_step / 12.0) * (u * dx + v * dy + wv * dz)
                    if f == 2:
                        new = new + time_step * get(3, start, stop)
                    elif f == 3:
                        new = new - time_step * wv
                    if kind == "rest":
                        out[0, k, z, start:stop, seg] = new.astype(jnp.bfloat16)
                    news.append(new)
                if kind == "mid":
                    out[0, k, z, :, seg] = jnp.concatenate(news, axis=0).astype(jnp.bfloat16)
                elif kind == "edge":
                    held[z, :, seg] = jnp.concatenate(news, axis=0).astype(jnp.bfloat16)
                    inner = mid[0, k, z, :, seg].astype(jnp.float32)
                    out[0, k, z, :, seg] = jnp.concatenate([news[0], inner, news[1]], axis=0).astype(jnp.bfloat16)
            return carry

        lax.fori_loop(0, depth, level, 0)
        part = cols // parts
        for j, send in enumerate(sends):
            at = pl.ds(pl.multiple_of(me_ref[j] * part, part), part)
            send[0, k] = held[:, :, at] if kind == "edge" else out[0, k, :, :, at]


def run_step(kind, first, members, parts, spans, order, state, lo=None, hi=None, mid=None, prior=None):
    _, _, levels, rows, cols = state.shape
    chunks = levels // depth
    fb = first // 2
    m0, m1 = members
    a = stencil_matrix(levels, rows, spans, kind != "mid")
    count = sum(stop - start for start, stop in spans)
    sds = jax.ShapeDtypeStruct
    in_specs = [
        pl.BlockSpec((1,) + a.shape[1:], lambda m, c, me: (c, 0, 0)),
        pl.BlockSpec((2 * wide, 2 * wide), lambda m, c, me: (0, 0)),
        pl.BlockSpec((1, 4, depth, rows, cols), lambda m, c, me: (m + m0, 0, c, 0, 0)),
        pl.BlockSpec((1, 2, 1, rows, cols), lambda m, c, me: (m + m0, fb, jnp.maximum(c * depth - 1, 0), 0, 0)),
        pl.BlockSpec((1, 2, 1, rows, cols), lambda m, c, me: (m + m0, fb, jnp.minimum(c * depth + depth, levels - 1), 0, 0)),
    ]
    args = [order, a, column_matrix(), state, state, state]
    if kind != "mid":
        in_specs += [pl.BlockSpec((1, 2, 2 * levels, cols), lambda m, c, me: (m + m0, fb, 0, 0))] * 2
        args += [lo, hi]
    if kind == "edge":
        in_specs.append(pl.BlockSpec((1, 2, depth, rows - count, cols), lambda m, c, me: (m, 0, c, 0, 0)))
        args.append(mid)
    alias = {}
    if prior is not None:
        alias = {len(args): 0}
        args.append(prior)
        in_specs.append(pl.BlockSpec(memory_space=pl.ANY))
    if kind == "mid":
        out_shape = [sds((m1 - m0, 2, levels, count, cols), state.dtype)]
        out_specs = [pl.BlockSpec((1, 2, depth, count, cols), lambda m, c, me: (m, 0, c, 0, 0))]
    else:
        out_shape = [sds(state.shape, state.dtype)]
        out_specs = [pl.BlockSpec((1, 2, depth, rows, cols), lambda m, c, me: (m + m0, fb, c, 0, 0))]
    if kind != "rest":
        out_shape += [sds((m1 - m0, 2, levels, count, cols // parts), state.dtype)] * parts
        out_specs += [pl.BlockSpec((1, 2, depth, count, cols // parts), lambda m, c, me: (m, 0, c, 0, 0))] * parts
    scratch = [
        pltpu.VMEM((3 * depth * count, cols), jnp.float32),
        pltpu.VMEM((depth * rows, 2 * cols), jnp.float32),
    ]
    if kind == "edge":
        scratch.insert(0, pltpu.VMEM((depth, count, cols), jnp.bfloat16))
    share = (m1 - m0) * count
    return pl.pallas_call(
        functools.partial(step_kernel, kind, first, parts, spans),
        out_shape=out_shape,
        grid_spec=pltpu.PrefetchScalarGridSpec(
            num_scalar_prefetch=1, grid=(m1 - m0, chunks), in_specs=in_specs, out_specs=out_specs, scratch_shapes=scratch
        ),
        input_output_aliases=alias,
        compiler_params=pltpu.CompilerParams(vmem_limit_bytes=vmem),
        cost_estimate=pl.CostEstimate(flops=share * 4 * 10**8, bytes_accessed=share * 2**18, transcendentals=0),
    )(*args)


def correlate_kernel(count, *refs):
    out = refs[-1]
    n = (len(refs) - 1) // 2
    inv = 1.0 / count

    def rows_of(blocks, z):
        sums = None
        for ref in blocks:
            for m in range(ref.shape[0]):
                w = ref[m, 0, z].astype(jnp.float32)
                b = ref[m, 1, z].astype(jnp.float32)
                terms = (b, w, b * b, w * w, b * w)
                sums = terms if sums is None else [p + q for p, q in zip(sums, terms)]
        mb, mw = sums[0] * inv, sums[1] * inv
        vb = sums[2] * inv - mb * mb
        vw = sums[3] * inv - mw * mw
        cov = sums[4] * inv - mb * mw
        return cov * lax.rsqrt(jnp.maximum(vb, var_floor) * jnp.maximum(vw, var_floor))

    for z in range(out.shape[0]):
        inner = rows_of(refs[:n], z)
        outer = rows_of(refs[n:-1], z)
        out[z] = jnp.concatenate([outer[:edge], inner, outer[edge:]], axis=0)


def run_correlate(count, mids, edges):
    _, _, levels, middle, part = mids[0].shape
    rows = middle + 2 * edge
    specs = [pl.BlockSpec(b.shape[:2] + (depth,) + b.shape[3:], lambda c: (0, 0, c, 0, 0)) for b in mids + edges]
    return pl.pallas_call(
        functools.partial(correlate_kernel, count),
        out_shape=jax.ShapeDtypeStruct((levels, rows, part), jnp.float32),
        grid=(levels // depth,),
        in_specs=specs,
        out_specs=pl.BlockSpec((depth, rows, part), lambda c: (c, 0, 0)),
        compiler_params=pltpu.CompilerParams(vmem_limit_bytes=vmem),
        cost_estimate=pl.CostEstimate(flops=10**8, bytes_accessed=5 * 2**20, transcendentals=0),
    )(*mids, *edges)


def partner(i, k, parts):
    if parts & (parts - 1) == 0:
        return i ^ k
    return (i + k) % parts


def on_device(parts, count, state):
    m_, _, levels, rows, cols = state.shape
    head = state[:, :, :, :2, :].reshape(m_, 4, 2 * levels, cols)
    tail = state[:, :, :, rows - 2 :, :].reshape(m_, 4, 2 * levels, cols)
    lo = lax.ppermute(tail, "space", [(i, (i + 1) % count) for i in range(count)])
    hi = lax.ppermute(head, "space", [((i + 1) % count, i) for i in range(count)])
    me = lax.axis_index("member")
    order = jnp.stack([jnp.asarray(partner(me, k, parts), jnp.int32) for k in range(parts)])

    def exchange(blocks):
        got = [blocks[0]]
        for k in range(1, parts):
            got.append(lax.ppermute(blocks[k], "member", [(i, partner(i, k, parts)) for i in range(parts)]))
        return got

    inner = ((edge, rows - edge),)
    outer = ((0, edge), (rows - edge, rows))
    halves = tuple((x, x + 16) for x in range(0, rows, 16))
    both = (0, m_)
    middle, *blocks = run_step("mid", 2, both, parts, inner, order, state)
    mids = exchange(blocks)
    stepped, *blocks = run_step("edge", 2, both, parts, outer, order, state, lo, hi, middle)
    edges = exchange(blocks)
    (stepped,) = run_step("rest", 0, both, parts, halves, order, state, lo, hi, None, stepped)
    return stepped, run_correlate(float(m_ * parts), mids, edges)


def solution(mesh):
    in_specs = (P("member", None, None, "space", None),)
    out_specs = (P("member", None, None, "space", None), P(None, "space", "member"))
    return jax.shard_map(
        functools.partial(on_device, mesh.shape["member"], mesh.shape["space"]),
        mesh=mesh, in_specs=in_specs, out_specs=out_specs, check_vma=False,
    )
```

```python
import functools

import jax
import jax.numpy as jnp
import numpy as np
from jax import lax
from jax.experimental import pallas as pl
from jax.experimental.pallas import tpu as pltpu
from jax.sharding import PartitionSpec as P

time_step = 0.2
viscosity = 0.1
var_floor = 0.25
depth = 4
edge = 8
wide = 256
vmem = 50 * 2**20


def stencil_matrix(levels, rows, spans, halos):
    chunks = levels // depth
    inner = (depth + 2) * rows
    xs = [x for start, stop in spans for x in range(start, stop)]
    a = np.zeros((chunks, 3, depth, len(xs), inner + (4 * levels if halos else 0)), np.float32)

    def column(c, z, x):
        if x < 0:
            return inner + (c * depth + z) * 2 + x + 2
        if x >= rows:
            return inner + 2 * levels + (c * depth + z) * 2 + x - rows
        return (z + 1) * rows + x

    for c in range(chunks):
        for z in range(depth):
            for n, x in enumerate(xs):
                for d, coef in ((1, 8), (-1, -8), (2, -1), (-2, 1)):
                    a[c, 0, z, n, column(c, z, x + d)] += coef
                a[c, 2, z, n, column(c, z, x + 1)] += 1
                a[c, 2, z, n, column(c, z, x - 1)] += 1
                a[c, 2, z, n, column(c, z, x)] += 44
                for d in (1, -1):
                    if 0 <= c * depth + z + d < levels:
                        a[c, 1, z, n, (z + 1 + d) * rows + x] += 6 * d
                        a[c, 2, z, n, (z + 1 + d) * rows + x] += 1
    return jnp.asarray(a.reshape(chunks, 3 * depth * len(xs), -1).astype(jnp.bfloat16))


def column_matrix():
    b = np.zeros((2 * wide, 2 * wide), np.float32)
    for n in range(wide):
        for d, coef in ((1, 8), (-1, -8), (2, -1), (-2, 1)):
            y = n + d
            row = y + wide + 128 if y < 0 else y if y < wide else y + 128
            b[row, n] += coef
            if d * d == 1:
                b[row, wide + n] += 1
    return jnp.asarray(b.astype(jnp.bfloat16))


def step_kernel(kind, first, parts, spans, me_ref, a_ref, b_ref, main, below, above, *rest):
    rest = list(rest)
    halos = [rest.pop(0), rest.pop(0)] if kind != "mid" else []
    mid = rest.pop(0) if kind == "edge" else None
    resy = rest.pop()
    res = rest.pop()
    held = rest.pop() if kind == "edge" else None
    if kind in ("edge", "full"):
        out, sends = rest[-1 - parts], rest[-parts:]
    elif kind == "mid":
        out, sends = rest[0], rest[1:]
    else:
        out, sends = rest[-1], []
    rows, cols = main.shape[3], main.shape[4]
    count = sum(stop - start for start, stop in spans)
    total = depth * count
    blocks = []
    for k in range(2):
        m = jnp.concatenate([main[0, first + k, z] for z in range(depth)], axis=0)
        for j in range(cols // wide):
            lo = (j * wide - 128) % cols
            hi = (j * wide + wide) % cols
            blocks.append(jnp.concatenate([m[:, j * wide : (j + 1) * wide], m[:, lo : lo + 128], m[:, hi : hi + 128]], axis=1))
    resy[...] = jnp.dot(jnp.concatenate(blocks, axis=0), b_ref[...], preferred_element_type=jnp.float32)
    for k in range(2):
        f = first + k
        m = jnp.concatenate([main[0, f, z] for z in range(depth)], axis=0)
        w = jnp.concatenate([below[0, k, 0], m, above[0, k, 0]] + [h[0, k] for h in halos], axis=0)
        res[...] = jnp.dot(a_ref[0], w, preferred_element_type=jnp.float32)
        def level(z, carry):
            for j in range(cols // wide):
                seg = slice(j * wide, (j + 1) * wide)

                def get(g, start, stop):
                    if kind in ("rest", "full"):
                        return main[0, g, z, start:stop, seg].astype(jnp.float32)
                    return main[0, g, z, :, seg].astype(jnp.float32)[start:stop]

                news = []
                at = 0
                for start, stop in spans:
                    base = pl.multiple_of(z * count + at, 8)
                    row = pl.multiple_of((k * (cols // wide) + j) * depth * rows + z * rows + start, 8)
                    size = stop - start
                    at += size
                    u, v, wv = get(0, start, stop), get(1, start, stop), get(2, start, stop)
                    dx = res[pl.ds(base, size), seg]
                    dz = res[pl.ds(pl.multiple_of(total + base, 8), size), seg]
                    lap = res[pl.ds(pl.multiple_of(2 * total + base, 8), size), seg]
                    dy = resy[pl.ds(row, size), :wide]
                    lap = lap + resy[pl.ds(row, size), wide:]
                    new = (time_step * viscosity) * lap - (time_step / 12.0) * (u * dx + v * dy + wv * dz)
                    if f == 2:
                        new = new + time_step * get(3, start, stop)
                    elif f == 3:
                        new = new - time_step * wv
                    if kind in ("rest", "full"):
                        out[0, k, z, start:stop, seg] = new.astype(jnp.bfloat16)
                    news.append(new)
                if kind == "mid":
                    out[0, k, z, :, seg] = jnp.concatenate(news, axis=0).astype(jnp.bfloat16)
                elif kind == "edge":
                    held[z, :, seg] = jnp.concatenate(news, axis=0).astype(jnp.bfloat16)
                    inner = mid[0, k, z, :, seg].astype(jnp.float32)
                    out[0, k, z, :, seg] = jnp.concatenate([news[0], inner, news[1]], axis=0).astype(jnp.bfloat16)
            return carry

        lax.fori_loop(0, depth, level, 0)
        part = cols // parts
        for j, send in enumerate(sends):
            at = pl.ds(pl.multiple_of(me_ref[j] * part, part), part)
            send[0, k] = held[:, :, at] if kind == "edge" else out[0, k, :, :, at]


def run_step(kind, first, members, parts, spans, order, state, lo=None, hi=None, mid=None, prior=None):
    _, _, levels, rows, cols = state.shape
    chunks = levels // depth
    fb = first // 2
    m0, m1 = members
    a = stencil_matrix(levels, rows, spans, kind != "mid")
    count = sum(stop - start for start, stop in spans)
    sds = jax.ShapeDtypeStruct
    in_specs = [
        pl.BlockSpec((1,) + a.shape[1:], lambda m, c, me: (c, 0, 0)),
        pl.BlockSpec((2 * wide, 2 * wide), lambda m, c, me: (0, 0)),
        pl.BlockSpec((1, 4, depth, rows, cols), lambda m, c, me: (m + m0, 0, c, 0, 0)),
        pl.BlockSpec((1, 2, 1, rows, cols), lambda m, c, me: (m + m0, fb, jnp.maximum(c * depth - 1, 0), 0, 0)),
        pl.BlockSpec((1, 2, 1, rows, cols), lambda m, c, me: (m + m0, fb, jnp.minimum(c * depth + depth, levels - 1), 0, 0)),
    ]
    args = [order, a, column_matrix(), state, state, state]
    if kind != "mid":
        in_specs += [pl.BlockSpec((1, 2, 2 * levels, cols), lambda m, c, me: (m + m0, fb, 0, 0))] * 2
        args += [lo, hi]
    if kind == "edge":
        in_specs.append(pl.BlockSpec((1, 2, depth, rows - count, cols), lambda m, c, me: (m, 0, c, 0, 0)))
        args.append(mid)
    alias = {}
    if prior is not None:
        alias = {len(args): 0}
        args.append(prior)
        in_specs.append(pl.BlockSpec(memory_space=pl.ANY))
    if kind == "mid":
        out_shape = [sds((m1 - m0, 2, levels, count, cols), state.dtype)]
        out_specs = [pl.BlockSpec((1, 2, depth, count, cols), lambda m, c, me: (m, 0, c, 0, 0))]
    else:
        out_shape = [sds(state.shape, state.dtype)]
        out_specs = [pl.BlockSpec((1, 2, depth, rows, cols), lambda m, c, me: (m + m0, fb, c, 0, 0))]
    if kind != "rest":
        out_shape += [sds((m1 - m0, 2, levels, count, cols // parts), state.dtype)] * parts
        out_specs += [pl.BlockSpec((1, 2, depth, count, cols // parts), lambda m, c, me: (m, 0, c, 0, 0))] * parts
    scratch = [
        pltpu.VMEM((3 * depth * count, cols), jnp.float32),
        pltpu.VMEM((2 * (cols // wide) * depth * rows, 2 * wide), jnp.float32),
    ]
    if kind == "edge":
        scratch.insert(0, pltpu.VMEM((depth, count, cols), jnp.bfloat16))
    share = (m1 - m0) * count
    return pl.pallas_call(
        functools.partial(step_kernel, kind, first, parts, spans),
        out_shape=out_shape,
        grid_spec=pltpu.PrefetchScalarGridSpec(
            num_scalar_prefetch=1, grid=(m1 - m0, chunks), in_specs=in_specs, out_specs=out_specs, scratch_shapes=scratch
        ),
        input_output_aliases=alias,
        compiler_params=pltpu.CompilerParams(vmem_limit_bytes=vmem),
        cost_estimate=pl.CostEstimate(flops=share * 4 * 10**8, bytes_accessed=share * 2**18, transcendentals=0),
    )(*args)


def correlate_kernel(count, n, *refs):
    out = refs[-1]
    inv = 1.0 / count

    def fields(z):
        for middle, outer in zip(refs[:n], refs[n : 2 * n]):
            for m in range(middle.shape[0]):
                pair = []
                for k in range(2):
                    o = outer[m, k, z].astype(jnp.float32)
                    pair.append(jnp.concatenate([o[:edge], middle[m, k, z].astype(jnp.float32), o[edge:]], axis=0))
                yield pair
        for whole in refs[2 * n : -1]:
            for m in range(whole.shape[0]):
                yield whole[m, 0, z].astype(jnp.float32), whole[m, 1, z].astype(jnp.float32)

    for z in range(out.shape[0]):
        sums = None
        for w, b in fields(z):
            terms = (b, w, b * b, w * w, b * w)
            sums = terms if sums is None else [p + q for p, q in zip(sums, terms)]
        mb, mw = sums[0] * inv, sums[1] * inv
        vb = sums[2] * inv - mb * mb
        vw = sums[3] * inv - mw * mw
        cov = sums[4] * inv - mb * mw
        out[z] = cov * lax.rsqrt(jnp.maximum(vb, var_floor) * jnp.maximum(vw, var_floor))


def run_correlate(count, mids, edges, wholes):
    _, _, levels, middle, part = mids[0].shape
    rows = middle + 2 * edge
    args = mids + edges + wholes
    return pl.pallas_call(
        functools.partial(correlate_kernel, count, len(mids)),
        out_shape=jax.ShapeDtypeStruct((levels, rows, part), jnp.float32),
        grid=(levels // depth,),
        in_specs=[pl.BlockSpec(b.shape[:2] + (depth,) + b.shape[3:], lambda c: (0, 0, c, 0, 0)) for b in args],
        out_specs=pl.BlockSpec((depth, rows, part), lambda c: (c, 0, 0)),
        compiler_params=pltpu.CompilerParams(vmem_limit_bytes=vmem),
        cost_estimate=pl.CostEstimate(flops=10**8, bytes_accessed=5 * 2**20, transcendentals=0),
    )(*args)


def partner(i, k, parts):
    if parts & (parts - 1) == 0:
        return i ^ k
    return (i + k) % parts


def on_device(parts, count, state):
    m_, _, levels, rows, cols = state.shape
    head = state[:, :, :, :2, :].reshape(m_, 4, 2 * levels, cols)
    tail = state[:, :, :, rows - 2 :, :].reshape(m_, 4, 2 * levels, cols)
    lo = lax.ppermute(tail, "space", [(i, (i + 1) % count) for i in range(count)])
    hi = lax.ppermute(head, "space", [((i + 1) % count, i) for i in range(count)])
    me = lax.axis_index("member")
    order = jnp.stack([jnp.asarray(partner(me, k, parts), jnp.int32) for k in range(parts)])

    def exchange(blocks):
        got = [blocks[0]]
        for k in range(1, parts):
            got.append(lax.ppermute(blocks[k], "member", [(i, partner(i, k, parts)) for i in range(parts)]))
        return got

    inner = ((edge, rows - edge),)
    outer = ((0, edge), (rows - edge, rows))
    halves = tuple((x, x + 16) for x in range(0, rows, 16))
    middle, *blocks = run_step("mid", 2, (0, 1), parts, inner, order, state)
    mids = exchange(blocks)
    stepped, *blocks = run_step("edge", 2, (0, 1), parts, outer, order, state, lo, hi, middle)
    edges = exchange(blocks)
    wholes = []
    if m_ > 1:
        stepped, *blocks = run_step("full", 2, (1, m_), parts, halves, order, state, lo, hi, None, stepped)
        wholes = exchange(blocks)
    (stepped,) = run_step("rest", 0, (0, m_), parts, halves, order, state, lo, hi, None, stepped)
    return stepped, run_correlate(float(m_ * parts), mids, edges, wholes)


def solution(mesh):
    in_specs = (P("member", None, None, "space", None),)
    out_specs = (P("member", None, None, "space", None), P(None, "space", "member"))
    return jax.shard_map(
        functools.partial(on_device, mesh.shape["member"], mesh.shape["space"]),
        mesh=mesh, in_specs=in_specs, out_specs=out_specs, check_vma=False,
    )
```

```python
import functools

import jax
import jax.numpy as jnp
import numpy as np
from jax import lax
from jax.experimental import pallas as pl
from jax.experimental.pallas import tpu as pltpu
from jax.sharding import PartitionSpec as P

time_step = 0.2
viscosity = 0.1
var_floor = 0.25
depth = 4
edge = 8
wide = 256
vmem = 50 * 2**20


def stencil_matrix(levels, rows, spans, halos):
    chunks = levels // depth
    inner = (depth + 2) * rows
    xs = [x for start, stop in spans for x in range(start, stop)]
    a = np.zeros((chunks, 3, depth, len(xs), inner + (4 * levels if halos else 0)), np.float32)

    def column(c, z, x):
        if x < 0:
            return inner + (c * depth + z) * 2 + x + 2
        if x >= rows:
            return inner + 2 * levels + (c * depth + z) * 2 + x - rows
        return (z + 1) * rows + x

    for c in range(chunks):
        for z in range(depth):
            for n, x in enumerate(xs):
                for d, coef in ((1, 8), (-1, -8), (2, -1), (-2, 1)):
                    a[c, 0, z, n, column(c, z, x + d)] += coef
                a[c, 2, z, n, column(c, z, x + 1)] += 1
                a[c, 2, z, n, column(c, z, x - 1)] += 1
                a[c, 2, z, n, column(c, z, x)] += 44
                for d in (1, -1):
                    if 0 <= c * depth + z + d < levels:
                        a[c, 1, z, n, (z + 1 + d) * rows + x] += 6 * d
                        a[c, 2, z, n, (z + 1 + d) * rows + x] += 1
    return jnp.asarray(a.reshape(chunks, 3 * depth * len(xs), -1).astype(jnp.bfloat16))


def column_matrix():
    b = np.zeros((2 * wide, 2 * wide), np.float32)
    for n in range(wide):
        for d, coef in ((1, 8), (-1, -8), (2, -1), (-2, 1)):
            y = n + d
            row = y + wide + 128 if y < 0 else y if y < wide else y + 128
            b[row, n] += coef
            if d * d == 1:
                b[row, wide + n] += 1
    return jnp.asarray(b.astype(jnp.bfloat16))


def step_kernel(kind, first, parts, spans, me_ref, a_ref, b_ref, main, below, above, *rest):
    rest = list(rest)
    halos = [rest.pop(0), rest.pop(0)] if kind != "mid" else []
    mid = rest.pop(0) if kind == "edge" else None
    resy = rest.pop()
    res = rest.pop()
    held = rest.pop() if kind == "edge" else None
    if kind in ("edge", "full"):
        out, sends = rest[-1 - parts], rest[-parts:]
    elif kind == "mid":
        out, sends = rest[0], rest[1:]
    else:
        out, sends = rest[-1], []
    rows, cols = main.shape[3], main.shape[4]
    count = sum(stop - start for start, stop in spans)
    total = depth * count
    blocks = []
    for k in range(2):
        m = jnp.concatenate([main[0, first + k, z] for z in range(depth)], axis=0)
        for j in range(cols // wide):
            lo = (j * wide - 128) % cols
            hi = (j * wide + wide) % cols
            blocks.append(jnp.concatenate([m[:, j * wide : (j + 1) * wide], m[:, lo : lo + 128], m[:, hi : hi + 128]], axis=1))
    resy[...] = jnp.dot(jnp.concatenate(blocks, axis=0), b_ref[...], preferred_element_type=jnp.float32)
    for k in range(2):
        m = jnp.concatenate([main[0, first + k, z] for z in range(depth)], axis=0)
        w = jnp.concatenate([below[0, k, 0], m, above[0, k, 0]] + [h[0, k] for h in halos], axis=0)
        res[k] = jnp.dot(a_ref[0], w, preferred_element_type=jnp.float32)
    for k in range(2):
        f = first + k

        def level(z):
            for j in range(cols // wide):
                seg = slice(j * wide, (j + 1) * wide)

                def get(g, start, stop):
                    if kind in ("rest", "full"):
                        return main[0, g, z, start:stop, seg].astype(jnp.float32)
                    return main[0, g, z, :, seg].astype(jnp.float32)[start:stop]

                news = []
                at = 0
                for start, stop in spans:
                    base = z * count + at
                    row = (k * (cols // wide) + j) * depth * rows + z * rows + start
                    size = stop - start
                    at += size
                    u, v, wv = get(0, start, stop), get(1, start, stop), get(2, start, stop)
                    dx = res[k, pl.ds(base, size), seg]
                    dz = res[k, pl.ds(total + base, size), seg]
                    lap = res[k, pl.ds(2 * total + base, size), seg]
                    dy = resy[pl.ds(row, size), :wide]
                    lap = lap + resy[pl.ds(row, size), wide:]
                    new = (time_step * viscosity) * lap - (time_step / 12.0) * (u * dx + v * dy + wv * dz)
                    if f == 2:
                        new = new + time_step * get(3, start, stop)
                    elif f == 3:
                        new = new - time_step * wv
                    if kind in ("rest", "full"):
                        out[0, k, z, start:stop, seg] = new.astype(jnp.bfloat16)
                    news.append(new)
                if kind == "mid":
                    out[0, k, z, :, seg] = jnp.concatenate(news, axis=0).astype(jnp.bfloat16)
                elif kind == "edge":
                    held[z, :, seg] = jnp.concatenate(news, axis=0).astype(jnp.bfloat16)
                    inner = mid[0, k, z, :, seg].astype(jnp.float32)
                    out[0, k, z, :, seg] = jnp.concatenate([news[0], inner, news[1]], axis=0).astype(jnp.bfloat16)

        for z in range(depth):
            level(z)
        part = cols // parts
        for j, send in enumerate(sends):
            at = pl.ds(pl.multiple_of(me_ref[j] * part, part), part)
            send[0, k] = held[:, :, at] if kind == "edge" else out[0, k, :, :, at]


def run_step(kind, first, members, parts, spans, order, state, lo=None, hi=None, mid=None, prior=None):
    _, _, levels, rows, cols = state.shape
    chunks = levels // depth
    fb = first // 2
    m0, m1 = members
    a = stencil_matrix(levels, rows, spans, kind != "mid")
    count = sum(stop - start for start, stop in spans)
    sds = jax.ShapeDtypeStruct
    in_specs = [
        pl.BlockSpec((1,) + a.shape[1:], lambda m, c, me: (c, 0, 0)),
        pl.BlockSpec((2 * wide, 2 * wide), lambda m, c, me: (0, 0)),
        pl.BlockSpec((1, 4, depth, rows, cols), lambda m, c, me: (m + m0, 0, c, 0, 0)),
        pl.BlockSpec((1, 2, 1, rows, cols), lambda m, c, me: (m + m0, fb, jnp.maximum(c * depth - 1, 0), 0, 0)),
        pl.BlockSpec((1, 2, 1, rows, cols), lambda m, c, me: (m + m0, fb, jnp.minimum(c * depth + depth, levels - 1), 0, 0)),
    ]
    args = [order, a, column_matrix(), state, state, state]
    if kind != "mid":
        in_specs += [pl.BlockSpec((1, 2, 2 * levels, cols), lambda m, c, me: (m + m0, fb, 0, 0))] * 2
        args += [lo, hi]
    if kind == "edge":
        in_specs.append(pl.BlockSpec((1, 2, depth, rows - count, cols), lambda m, c, me: (m, 0, c, 0, 0)))
        args.append(mid)
    alias = {}
    if prior is not None:
        alias = {len(args): 0}
        args.append(prior)
        in_specs.append(pl.BlockSpec(memory_space=pl.ANY))
    if kind == "mid":
        out_shape = [sds((m1 - m0, 2, levels, count, cols), state.dtype)]
        out_specs = [pl.BlockSpec((1, 2, depth, count, cols), lambda m, c, me: (m, 0, c, 0, 0))]
    else:
        out_shape = [sds(state.shape, state.dtype)]
        out_specs = [pl.BlockSpec((1, 2, depth, rows, cols), lambda m, c, me: (m + m0, fb, c, 0, 0))]
    if kind != "rest":
        out_shape += [sds((m1 - m0, 2, levels, count, cols // parts), state.dtype)] * parts
        out_specs += [pl.BlockSpec((1, 2, depth, count, cols // parts), lambda m, c, me: (m, 0, c, 0, 0))] * parts
    scratch = [
        pltpu.VMEM((2, 3 * depth * count, cols), jnp.float32),
        pltpu.VMEM((2 * (cols // wide) * depth * rows, 2 * wide), jnp.float32),
    ]
    if kind == "edge":
        scratch.insert(0, pltpu.VMEM((depth, count, cols), jnp.bfloat16))
    share = (m1 - m0) * count
    return pl.pallas_call(
        functools.partial(step_kernel, kind, first, parts, spans),
        out_shape=out_shape,
        grid_spec=pltpu.PrefetchScalarGridSpec(
            num_scalar_prefetch=1, grid=(m1 - m0, chunks), in_specs=in_specs, out_specs=out_specs, scratch_shapes=scratch
        ),
        input_output_aliases=alias,
        compiler_params=pltpu.CompilerParams(vmem_limit_bytes=vmem),
        cost_estimate=pl.CostEstimate(flops=share * 4 * 10**8, bytes_accessed=share * 2**18, transcendentals=0),
    )(*args)


def correlate_kernel(count, n, *refs):
    out = refs[-1]
    inv = 1.0 / count

    def fields(z):
        for middle, outer in zip(refs[:n], refs[n : 2 * n]):
            for m in range(middle.shape[0]):
                pair = []
                for k in range(2):
                    o = outer[m, k, z].astype(jnp.float32)
                    pair.append(jnp.concatenate([o[:edge], middle[m, k, z].astype(jnp.float32), o[edge:]], axis=0))
                yield pair
        for whole in refs[2 * n : -1]:
            for m in range(whole.shape[0]):
                yield whole[m, 0, z].astype(jnp.float32), whole[m, 1, z].astype(jnp.float32)

    for z in range(out.shape[0]):
        sums = None
        for w, b in fields(z):
            terms = (b, w, b * b, w * w, b * w)
            sums = terms if sums is None else [p + q for p, q in zip(sums, terms)]
        mb, mw = sums[0] * inv, sums[1] * inv
        vb = sums[2] * inv - mb * mb
        vw = sums[3] * inv - mw * mw
        cov = sums[4] * inv - mb * mw
        out[z] = cov * lax.rsqrt(jnp.maximum(vb, var_floor) * jnp.maximum(vw, var_floor))


def run_correlate(count, mids, edges, wholes):
    _, _, levels, middle, part = mids[0].shape
    rows = middle + 2 * edge
    args = mids + edges + wholes
    return pl.pallas_call(
        functools.partial(correlate_kernel, count, len(mids)),
        out_shape=jax.ShapeDtypeStruct((levels, rows, part), jnp.float32),
        grid=(levels // depth,),
        in_specs=[pl.BlockSpec(b.shape[:2] + (depth,) + b.shape[3:], lambda c: (0, 0, c, 0, 0)) for b in args],
        out_specs=pl.BlockSpec((depth, rows, part), lambda c: (c, 0, 0)),
        compiler_params=pltpu.CompilerParams(vmem_limit_bytes=vmem),
        cost_estimate=pl.CostEstimate(flops=10**8, bytes_accessed=5 * 2**20, transcendentals=0),
    )(*args)


def partner(i, k, parts):
    if parts & (parts - 1) == 0:
        return i ^ k
    return (i + k) % parts


def on_device(parts, count, state):
    m_, _, levels, rows, cols = state.shape
    head = state[:, :, :, :2, :].reshape(m_, 4, 2 * levels, cols)
    tail = state[:, :, :, rows - 2 :, :].reshape(m_, 4, 2 * levels, cols)
    lo = lax.ppermute(tail, "space", [(i, (i + 1) % count) for i in range(count)])
    hi = lax.ppermute(head, "space", [((i + 1) % count, i) for i in range(count)])
    me = lax.axis_index("member")
    order = jnp.stack([jnp.asarray(partner(me, k, parts), jnp.int32) for k in range(parts)])

    def exchange(blocks):
        got = [blocks[0]]
        for k in range(1, parts):
            got.append(lax.ppermute(blocks[k], "member", [(i, partner(i, k, parts)) for i in range(parts)]))
        return got

    inner = ((edge, rows - edge),)
    outer = ((0, edge), (rows - edge, rows))
    halves = tuple((x, x + 16) for x in range(0, rows, 16))
    middle, *blocks = run_step("mid", 2, (0, 1), parts, inner, order, state)
    mids = exchange(blocks)
    stepped, *blocks = run_step("edge", 2, (0, 1), parts, outer, order, state, lo, hi, middle)
    edges = exchange(blocks)
    wholes = []
    if m_ > 1:
        stepped, *blocks = run_step("full", 2, (1, m_), parts, halves, order, state, lo, hi, None, stepped)
        wholes = exchange(blocks)
    (stepped,) = run_step("rest", 0, (0, m_), parts, halves, order, state, lo, hi, None, stepped)
    return stepped, run_correlate(float(m_ * parts), mids, edges, wholes)


def solution(mesh):
    in_specs = (P("member", None, None, "space", None),)
    out_specs = (P("member", None, None, "space", None), P(None, "space", "member"))
    return jax.shard_map(
        functools.partial(on_device, mesh.shape["member"], mesh.shape["space"]),
        mesh=mesh, in_specs=in_specs, out_specs=out_specs, check_vma=False,
    )
```

```python
import functools

import jax
import jax.numpy as jnp
import numpy as np
from jax import lax
from jax.experimental import pallas as pl
from jax.experimental.pallas import tpu as pltpu
from jax.sharding import PartitionSpec as P

time_step = 0.2
viscosity = 0.1
var_floor = 0.25
depth = 4
edge = 8
wide = 256
vmem = 50 * 2**20


def stencil_matrix(levels, rows, spans, halos):
    chunks = levels // depth
    inner = (depth + 2) * rows
    xs = [x for start, stop in spans for x in range(start, stop)]
    a = np.zeros((chunks, 3, depth, len(xs), inner + (4 * levels if halos else 0)), np.float32)

    def column(c, z, x):
        if x < 0:
            return inner + (c * depth + z) * 2 + x + 2
        if x >= rows:
            return inner + 2 * levels + (c * depth + z) * 2 + x - rows
        return (z + 1) * rows + x

    for c in range(chunks):
        for z in range(depth):
            for n, x in enumerate(xs):
                for d, coef in ((1, 8), (-1, -8), (2, -1), (-2, 1)):
                    a[c, 0, z, n, column(c, z, x + d)] += coef
                a[c, 2, z, n, column(c, z, x + 1)] += 1
                a[c, 2, z, n, column(c, z, x - 1)] += 1
                a[c, 2, z, n, column(c, z, x)] += 44
                for d in (1, -1):
                    if 0 <= c * depth + z + d < levels:
                        a[c, 1, z, n, (z + 1 + d) * rows + x] += 6 * d
                        a[c, 2, z, n, (z + 1 + d) * rows + x] += 1
    return jnp.asarray(a.reshape(chunks, 3 * depth * len(xs), -1).astype(jnp.bfloat16))


def column_matrix():
    b = np.zeros((2 * wide, 2 * wide), np.float32)
    for n in range(wide):
        for d, coef in ((1, 8), (-1, -8), (2, -1), (-2, 1)):
            y = n + d
            row = y + wide + 128 if y < 0 else y if y < wide else y + 128
            b[row, n] += coef
            if d * d == 1:
                b[row, wide + n] += 1
    return jnp.asarray(b.astype(jnp.bfloat16))


def step_kernel(kind, first, parts, spans, me_ref, a_ref, b_ref, main, below, above, *rest):
    rest = list(rest)
    halos = [rest.pop(0), rest.pop(0)] if kind != "mid" else []
    mid = rest.pop(0) if kind == "edge" else None
    resy = rest.pop()
    res = rest.pop()
    held = rest.pop() if kind == "edge" else None
    if kind in ("edge", "full"):
        out, sends = rest[-1 - parts], rest[-parts:]
    elif kind == "mid":
        out, sends = rest[0], rest[1:]
    else:
        out, sends = rest[-1], []
    rows, cols = main.shape[3], main.shape[4]
    count = sum(stop - start for start, stop in spans)
    total = depth * count
    blocks = []
    for k in range(2):
        m = jnp.concatenate([main[0, first + k, z] for z in range(depth)], axis=0)
        for j in range(cols // wide):
            lo = (j * wide - 128) % cols
            hi = (j * wide + wide) % cols
            blocks.append(jnp.concatenate([m[:, j * wide : (j + 1) * wide], m[:, lo : lo + 128], m[:, hi : hi + 128]], axis=1))
    resy[...] = jnp.dot(jnp.concatenate(blocks, axis=0), b_ref[...], preferred_element_type=jnp.float32)
    for k in range(2):
        m = jnp.concatenate([main[0, first + k, z] for z in range(depth)], axis=0)
        w = jnp.concatenate([below[0, k, 0], m, above[0, k, 0]] + [h[0, k] for h in halos], axis=0)
        res[k] = jnp.dot(a_ref[0], w, preferred_element_type=jnp.float32)
    for k in range(2):
        f = first + k

        def level(z):
            for j in range(cols // wide):
                seg = slice(j * wide, (j + 1) * wide)

                def get(g, start, stop):
                    if kind in ("rest", "full"):
                        return main[0, g, z, start:stop, seg].astype(jnp.float32)
                    return main[0, g, z, :, seg].astype(jnp.float32)[start:stop]

                news = []
                at = 0
                for start, stop in spans:
                    base = z * count + at
                    row = (k * (cols // wide) + j) * depth * rows + z * rows + start
                    size = stop - start
                    at += size
                    u, v, wv = get(0, start, stop), get(1, start, stop), get(2, start, stop)
                    dx = res[k, pl.ds(base, size), seg]
                    dz = res[k, pl.ds(total + base, size), seg]
                    lap = res[k, pl.ds(2 * total + base, size), seg]
                    dy = resy[pl.ds(row, size), :wide]
                    lap = lap + resy[pl.ds(row, size), wide:]
                    new = (time_step * viscosity) * lap - (time_step / 12.0) * (u * dx + v * dy + wv * dz)
                    if f == 2:
                        new = new + time_step * get(3, start, stop)
                    elif f == 3:
                        new = new - time_step * wv
                    if kind in ("rest", "full"):
                        out[0, k, z, start:stop, seg] = new.astype(jnp.bfloat16)
                    news.append(new)
                if kind == "mid":
                    out[0, k, z, :, seg] = jnp.concatenate(news, axis=0).astype(jnp.bfloat16)
                elif kind == "edge":
                    held[z, :, seg] = jnp.concatenate(news, axis=0).astype(jnp.bfloat16)
                    inner = mid[0, k, z, :, seg].astype(jnp.float32)
                    out[0, k, z, :, seg] = jnp.concatenate([news[0], inner, news[1]], axis=0).astype(jnp.bfloat16)

        for z in range(depth):
            level(z)
        part = cols // parts
        for j, send in enumerate(sends):
            at = pl.ds(pl.multiple_of(me_ref[j] * part, part), part)
            send[0, k] = held[:, :, at] if kind == "edge" else out[0, k, :, :, at]


def run_step(kind, first, members, parts, spans, order, state, lo=None, hi=None, mid=None, prior=None):
    _, _, levels, rows, cols = state.shape
    chunks = levels // depth
    fb = first // 2
    m0, m1 = members
    a = stencil_matrix(levels, rows, spans, kind != "mid")
    count = sum(stop - start for start, stop in spans)
    sds = jax.ShapeDtypeStruct
    in_specs = [
        pl.BlockSpec((1,) + a.shape[1:], lambda m, c, me: (c, 0, 0)),
        pl.BlockSpec((2 * wide, 2 * wide), lambda m, c, me: (0, 0)),
        pl.BlockSpec((1, 4, depth, rows, cols), lambda m, c, me: (m + m0, 0, c, 0, 0)),
        pl.BlockSpec((1, 2, 1, rows, cols), lambda m, c, me: (m + m0, fb, jnp.maximum(c * depth - 1, 0), 0, 0)),
        pl.BlockSpec((1, 2, 1, rows, cols), lambda m, c, me: (m + m0, fb, jnp.minimum(c * depth + depth, levels - 1), 0, 0)),
    ]
    args = [order, a, column_matrix(), state, state, state]
    if kind != "mid":
        in_specs += [pl.BlockSpec((1, 2, 2 * levels, cols), lambda m, c, me: (m + m0, fb, 0, 0))] * 2
        args += [lo, hi]
    if kind == "edge":
        in_specs.append(pl.BlockSpec((1, 2, depth, rows - count, cols), lambda m, c, me: (m, 0, c, 0, 0)))
        args.append(mid)
    alias = {}
    if prior is not None:
        alias = {len(args): 0}
        args.append(prior)
        in_specs.append(pl.BlockSpec(memory_space=pl.ANY))
    if kind == "mid":
        out_shape = [sds((m1 - m0, 2, levels, count, cols), state.dtype)]
        out_specs = [pl.BlockSpec((1, 2, depth, count, cols), lambda m, c, me: (m, 0, c, 0, 0))]
    else:
        out_shape = [sds(state.shape, state.dtype)]
        out_specs = [pl.BlockSpec((1, 2, depth, rows, cols), lambda m, c, me: (m + m0, fb, c, 0, 0))]
    if kind != "rest":
        out_shape += [sds((m1 - m0, 2, levels, count, cols // parts), state.dtype)] * parts
        out_specs += [pl.BlockSpec((1, 2, depth, count, cols // parts), lambda m, c, me: (m, 0, c, 0, 0))] * parts
    scratch = [
        pltpu.VMEM((2, 3 * depth * count, cols), jnp.float32),
        pltpu.VMEM((2 * (cols // wide) * depth * rows, 2 * wide), jnp.float32),
    ]
    if kind == "edge":
        scratch.insert(0, pltpu.VMEM((depth, count, cols), jnp.bfloat16))
    share = (m1 - m0) * count
    return pl.pallas_call(
        functools.partial(step_kernel, kind, first, parts, spans),
        out_shape=out_shape,
        grid_spec=pltpu.PrefetchScalarGridSpec(
            num_scalar_prefetch=1, grid=(m1 - m0, chunks), in_specs=in_specs, out_specs=out_specs, scratch_shapes=scratch
        ),
        input_output_aliases=alias,
        compiler_params=pltpu.CompilerParams(vmem_limit_bytes=vmem),
        cost_estimate=pl.CostEstimate(flops=share * 4 * 10**9, bytes_accessed=share * 2**18, transcendentals=0),
    )(*args)


def correlate_kernel(count, n, *refs):
    out = refs[-1]
    inv = 1.0 / count

    def fields(z):
        for middle, outer in zip(refs[:n], refs[n : 2 * n]):
            for m in range(middle.shape[0]):
                pair = []
                for k in range(2):
                    o = outer[m, k, z].astype(jnp.float32)
                    pair.append(jnp.concatenate([o[:edge], middle[m, k, z].astype(jnp.float32), o[edge:]], axis=0))
                yield pair
        for whole in refs[2 * n : -1]:
            for m in range(whole.shape[0]):
                yield whole[m, 0, z].astype(jnp.float32), whole[m, 1, z].astype(jnp.float32)

    for z in range(out.shape[0]):
        sums = None
        for w, b in fields(z):
            terms = (b, w, b * b, w * w, b * w)
            sums = terms if sums is None else [p + q for p, q in zip(sums, terms)]
        mb, mw = sums[0] * inv, sums[1] * inv
        vb = sums[2] * inv - mb * mb
        vw = sums[3] * inv - mw * mw
        cov = sums[4] * inv - mb * mw
        out[z] = cov * lax.rsqrt(jnp.maximum(vb, var_floor) * jnp.maximum(vw, var_floor))


def run_correlate(count, mids, edges, wholes):
    _, _, levels, middle, part = mids[0].shape
    rows = middle + 2 * edge
    args = mids + edges + wholes
    return pl.pallas_call(
        functools.partial(correlate_kernel, count, len(mids)),
        out_shape=jax.ShapeDtypeStruct((levels, rows, part), jnp.float32),
        grid=(levels // depth,),
        in_specs=[pl.BlockSpec(b.shape[:2] + (depth,) + b.shape[3:], lambda c: (0, 0, c, 0, 0)) for b in args],
        out_specs=pl.BlockSpec((depth, rows, part), lambda c: (c, 0, 0)),
        compiler_params=pltpu.CompilerParams(vmem_limit_bytes=vmem),
        cost_estimate=pl.CostEstimate(flops=10**8, bytes_accessed=5 * 2**20, transcendentals=0),
    )(*args)


def partner(i, k, parts):
    if parts & (parts - 1) == 0:
        return i ^ k
    return (i + k) % parts


def on_device(parts, count, state):
    m_, _, levels, rows, cols = state.shape
    head = state[:, :, :, :2, :].reshape(m_, 4, 2 * levels, cols)
    tail = state[:, :, :, rows - 2 :, :].reshape(m_, 4, 2 * levels, cols)
    lo = lax.ppermute(tail, "space", [(i, (i + 1) % count) for i in range(count)])
    hi = lax.ppermute(head, "space", [((i + 1) % count, i) for i in range(count)])
    me = lax.axis_index("member")
    order = jnp.stack([jnp.asarray(partner(me, k, parts), jnp.int32) for k in range(parts)])

    def exchange(blocks):
        got = [blocks[0]]
        for k in range(1, parts):
            got.append(lax.ppermute(blocks[k], "member", [(i, partner(i, k, parts)) for i in range(parts)]))
        return got

    inner = ((edge, rows - edge),)
    outer = ((0, edge), (rows - edge, rows))
    halves = tuple((x, x + 16) for x in range(0, rows, 16))
    middle, *blocks = run_step("mid", 2, (0, 1), parts, inner, order, state)
    mids = exchange(blocks)
    stepped, *blocks = run_step("edge", 2, (0, 1), parts, outer, order, state, lo, hi, middle)
    edges = exchange(blocks)
    wholes = []
    if m_ > 1:
        stepped, mids[1] = lax.optimization_barrier((stepped, mids[1]))
        stepped, *blocks = run_step("full", 2, (1, m_), parts, halves, order, state, lo, hi, None, stepped)
        wholes = exchange(blocks)
    (stepped,) = run_step("rest", 0, (0, m_), parts, halves, order, state, lo, hi, None, stepped)
    return stepped, run_correlate(float(m_ * parts), mids, edges, wholes)


def solution(mesh):
    in_specs = (P("member", None, None, "space", None),)
    out_specs = (P("member", None, None, "space", None), P(None, "space", "member"))
    return jax.shard_map(
        functools.partial(on_device, mesh.shape["member"], mesh.shape["space"]),
        mesh=mesh, in_specs=in_specs, out_specs=out_specs, check_vma=False,
    )
```
